32 devices in a mesh: batch: 2 (over x), space: 16 (over z, y, core).
Axes of the slice: x: 2, y: 2, z: 4, core: 2. Of those that a mesh axis runs over, the one named last changes fastest.
Arguments:
- courant: float32 [128, 16, 256], P('space'), may hold values from 0.06 to 0.18
- wavelet: float32 [2, 64, 7], P('batch'), may hold values from -6 to 6
- source_owner: int32 [2, 64], P('batch'), may hold values from 0 to 15
- source_cell: int32 [2, 64], P('batch'), may hold values from 0 to 32767
- traces: float32 [2, 4096, 7], P('batch', 'space'), may hold values from -6 to 6
- station_owner: int32 [2, 4096, 1], P('batch', 'space'), may hold values from 0 to 15; in each aligned block of 256 rows (0 to 255, 256 to 511, ..., all dimensions but the last counted through in order) at most 32 rows name the same one
- station_cell: int32 [2, 4096], P('batch', 'space'), may hold values from 0 to 32767
Outputs:
- update: float32 [128, 16, 256], P('space', 'batch')
- agreement: float32 [1], replicated
The draws below stay inside these ranges and needn't reach their ends.
Inputs may be any that keep to these rules, and one draw needn't show every extreme that they name: `station_owner`: among the 256 trace rows of one device, at most 32 name the same owner, and in every draw some device reaches 32 for some owner.
All inputs are finite; a program needn't handle non-finite values.
Results may differ from the reference program's by a relative error of at most 0.0003.
Values sent between devices are 32-bit elements; how exact they have to be, the bound alone decides.
A program may use at most 64 MiB of HBM per device.

```python
import math
import jax
import jax.numpy as jnp
import numpy as np

CX = 8
CY = 16
CZ = 256
STEPS = 7
STA_DEV = 256
BATCHES = 2
NX = 128
SRC = 64
STATIONS = 4096
CAP = 32
N_SPACE = 16


def set_ends(array, rng, least, largest):
    longest = array.shape.index(max(array.shape))
    spots = []
    for shift in (0, 1):
        where = [jax.random.randint(jax.random.fold_in(rng, axis), (), 0, length) for axis, length in enumerate(array.shape)]
        where[longest] = (where[longest] + shift) % array.shape[longest]
        spots.append(tuple(where))
    return array.at[spots[0]].set(least).at[spots[1]].set(largest)


def block_levels(key, shape, split, low, high):
    gain, own = 1.0, jax.random.fold_in(key, 6)
    for axis_at, parts in split:
        draws = jnp.exp(jax.random.uniform(jax.random.fold_in(own, axis_at), (parts,), jnp.float32, low / len(split), high / len(split)))
        gain = gain * jnp.repeat(draws, shape[axis_at] // parts).reshape([-1 if axis == axis_at else 1 for axis in range(len(shape))])
    return gain


def assign_block(stream_key, own, number, rows, number_of, top, bound, lean):
    order = jax.random.permutation(stream_key, number_of)
    packed, usual = portions_of(number_of, rows * top, bound, lean, True), portions_of(number_of, rows * top, bound, lean, False)
    places = jnp.arange(number_of)

    def named(sizes, offset_by):
        used = int((sizes > 0).sum())
        fixed = max(1, used // 4)
        shifted = fixed + (places - fixed + offset_by * (used - fixed)) % max(1, number_of - fixed)
        return jnp.zeros((number_of,), jnp.int32).at[order[jnp.where(places < fixed, places, shifted)]].set(jnp.asarray(sizes, jnp.int32))

    sizes = jnp.where(number % 4 == 0, named(packed, number // 4), named(usual, number - number // 4 - 1))
    mixed = jax.random.permutation(jax.random.fold_in(own, 3), number_of)
    giver, receiver = mixed[0:number_of // 2 * 2:2], mixed[1:number_of // 2 * 2:2]
    slack = jnp.minimum(sizes[giver] - 1, bound - sizes[receiver]) // 2
    slack = jnp.where((giver == order[0]) | (receiver == order[0]) | (sizes[receiver] == 0), 0, jnp.maximum(slack, 0))
    shifted = jax.random.randint(jax.random.fold_in(own, 4), (number_of // 2,), 0, 1 << 20) % (slack + 1)
    sizes = sizes.at[giver].add(-shifted).at[receiver].add(shifted)
    members = jnp.searchsorted(jnp.cumsum(sizes), jnp.arange(rows * top), side="right").astype(jnp.int32)
    grid = members.reshape(top, rows).T
    grid = grid[jax.random.permutation(jax.random.fold_in(own, 1), rows)]
    offset_by = jax.random.randint(jax.random.fold_in(own, 2), (rows, 1), 0, top)
    return jnp.take_along_axis(grid, (jnp.arange(top)[None, :] + offset_by) % top, axis=1)


def portions_of(amount, total, most, slope, full):
    weights = [(1 << 20) // math.isqrt(rank ** slope) + 1 for rank in range(1, amount + 1)]
    largest = most if full else min(most, max(-(-total // amount), total * weights[0] // sum(weights)))
    least = 1 if total - largest >= amount - 1 else 0
    holding, spare = [largest] + [least] * (amount - 1), total - largest - least * (amount - 1)
    while spare > 0:
        free = [i for i in range(1, amount) if holding[i] < largest] or [i for i in range(1, amount) if holding[i] < most]
        mass, remaining = sum([weights[i] for i in free]), spare
        for i in free:
            addition = min(most - holding[i], max(1, remaining * weights[i] // mass), spare)
            holding[i] = holding[i] + addition
            spare = spare - addition
    return np.array(holding)


def normal_values(key, extent, width, bound, pieces=(), kind=jnp.bfloat16):
    level = block_levels(key, extent, pieces, -0.22, 0.18) if pieces else 1.0
    values = jax.random.normal(key, extent, jnp.float32) * width * level
    return jnp.minimum(jnp.maximum(values, -bound), bound).astype(kind)


def setup_inputs(seed: int = 0) -> dict:
    splits = jax.random.split(jax.random.key(seed), 8)
    courant = jnp.clip(0.06 + 0.120000008 * jax.random.uniform(splits[0], (NX, CY, CZ), jnp.float32) ** block_levels(splits[0], (NX, CY, CZ), ((0, 16),), -0.2, 0.2), 0.06, 0.18)
    wavelet = normal_values(splits[1], (BATCHES, SRC, STEPS), 1.0, 6.0, ((0, 2),), jnp.float32)
    source_owner = set_ends(jax.random.randint(splits[2], (BATCHES, SRC), 0, N_SPACE), jax.random.fold_in(splits[2], 1), 0, N_SPACE - 1).astype(jnp.int32)
    source_cell = set_ends(jax.random.randint(splits[3], (BATCHES, SRC), 0, CX * CY * CZ), jax.random.fold_in(splits[3], 1), 0, (CX * CY * CZ) - 1).astype(jnp.int32)
    traces = normal_values(splits[4], (BATCHES, STATIONS, STEPS), 1.0, 6.0, ((0, 2), (1, 16)), jnp.float32)
    station_owner_keys = jax.random.split(jax.random.fold_in(splits[5], 1), BATCHES * STATIONS // STA_DEV)
    station_owner_turns = jax.random.permutation(jax.random.fold_in(splits[5], 3), BATCHES * STATIONS // STA_DEV)
    station_owner = jax.vmap(lambda own, number: assign_block(jax.random.fold_in(splits[5], 2), own, number, STA_DEV, N_SPACE, 1, CAP, 2))(station_owner_keys, station_owner_turns).reshape((BATCHES, STATIONS, 1))
    station_cell = set_ends(jax.random.randint(splits[6], (BATCHES, STATIONS), 0, CX * CY * CZ), jax.random.fold_in(splits[6], 1), 0, (CX * CY * CZ) - 1).astype(jnp.int32)
    return {"courant": courant, "wavelet": wavelet, "source_owner": source_owner, "source_cell": source_cell, "traces": traces, "station_owner": station_owner, "station_cell": station_cell}


center_tap = -205.0 / 72.0
stencil_taps = (1.6, -0.2, 8.0 / 315.0, -1.0 / 560.0)
epsilon = 1e-06

def laplace_rows(extended, height):
    span_y = extended.shape[1] - 8
    span_z = extended.shape[2] - 8

    def window(first, second, third):
        return extended[first:first + height, second:second + span_y, third:third + span_z]
    accumulated = 3.0 * center_tap * window(4, 4, 4)
    for offset in range(1, 5):
        neighbours = window(4 + offset, 4, 4) + window(4 - offset, 4, 4)
        neighbours = neighbours + window(4, 4 + offset, 4) + window(4, 4 - offset, 4)
        neighbours = neighbours + window(4, 4, 4 + offset) + window(4, 4, 4 - offset)
        accumulated = accumulated + stencil_taps[offset - 1] * neighbours
    return accumulated

def pad_all(wave_field):
    return jnp.pad(wave_field, ((4, 4), (4, 4), (4, 4)))

def inject(wave_field, positions, amounts):
    flattened = wave_field.reshape(-1)
    return flattened.at[positions].add(amounts).reshape(wave_field.shape)

def reference(courant, wavelet, source_owner, source_cell, traces, station_owner, station_cell):
    volume = CX * CY * CZ
    grid_shape = (NX, CY, CZ)
    gradients = []
    for member in range(BATCHES):
        source_flat = source_owner[member].astype(jnp.int32) * volume + source_cell[member].astype(jnp.int32)
        station_flat = station_owner[member, :, 0].astype(jnp.int32) * volume + station_cell[member].astype(jnp.int32)
        zero_field = jnp.zeros(grid_shape, jnp.float32)
        snapshots = [zero_field, inject(zero_field, source_flat, wavelet[member, :, 0])]
        for moment in range(1, STEPS):
            current = snapshots[moment]
            following = 2.0 * current - snapshots[moment - 1] + courant * laplace_rows(pad_all(current), NX)
            snapshots.append(inject(following, source_flat, wavelet[member, :, moment]))
        adjoint = inject(zero_field, station_flat, traces[member, :, STEPS - 1])
        previous_adjoint = zero_field
        gradient = adjoint * (snapshots[STEPS] - 2.0 * snapshots[STEPS - 1] + snapshots[STEPS - 2])
        for moment in range(STEPS - 2, 0, -1):
            newer = 2.0 * adjoint - previous_adjoint + laplace_rows(pad_all(courant * adjoint), NX)
            newer = inject(newer, station_flat, traces[member, :, moment])
            previous_adjoint, adjoint = (adjoint, newer)
            gradient = gradient + adjoint * (snapshots[moment + 1] - 2.0 * snapshots[moment] + snapshots[moment - 1])
        gradients.append(gradient)
    cells = float(NX * CY * CZ)
    mean_first = jnp.sum(gradients[0] * gradients[0]) / cells
    mean_second = jnp.sum(gradients[1] * gradients[1]) / cells
    update = (gradients[0] + gradients[1]) / jnp.sqrt((mean_first + mean_second) / 2.0 + epsilon)
    share = (mean_first + epsilon) / (mean_first + mean_second + 2.0 * epsilon)
    return (update, jnp.stack([share]))
```

```python
import functools
import jax
import jax.numpy as jnp
from jax import lax
from jax.experimental import pallas as pl
from jax.experimental.pallas import tpu as pltpu
from jax.sharding import PartitionSpec as P

center_tap = -205.0 / 72.0
stencil_taps = (1.6, -0.2, 8.0 / 315.0, -1.0 / 560.0)
epsilon = 1e-06
MESH = pl.DeviceIdType.MESH
F32, BF16, I32 = jnp.float32, jnp.bfloat16, jnp.int32
REACH = 3
HOPS = (-1, 1, -2, 2, -3, 3)


def halves_of(x):
    high = x.astype(BF16)
    return high, (x - high.astype(F32)).astype(BF16)


def dot(a, b):
    return lax.dot_general(a, b, (((1,), (0,)), ((), ())), preferred_element_type=F32)


def dot_lanes(a, b):
    return lax.dot_general(a, b, (((1,), (1,)), ((), ())), preferred_element_type=F32)


def taps_at(distance, middle):
    value = jnp.where(distance == 0, middle, 0.0)
    for k in range(4):
        value = jnp.where(distance == k + 1, stencil_taps[k], value)
    return value


def placed(row_ids, high, low, onehot, first, count):
    rows = lax.broadcasted_iota(I32, (count, row_ids.shape[1]), 0) + first
    here = rows == row_ids
    stacked = jnp.concatenate([jnp.where(here, high, 0.0), jnp.where(here, low, 0.0)], axis=0)
    both = dot_lanes(stacked.astype(BF16), onehot)
    return both[:count] + both[count:]


def kernel(
    parties, batches, steps, block, width_y, width_z, cap, rows,
    cour, wav, s_own, s_cell, tra, t_own, t_cell,
    upd, agr,
    vbuf, sbuf, rbuf, relay, cext, field_r, ua, ub, uh, ul, aa, ab, ah, al, dbuf,
    taps_xy, taps_z, gbuf, gin, nbuf,
    a2a_s, a2a_r, c_s, c_r, l_s, l_r, g_s, g_r, n_s, n_r,
):
    b = lax.axis_index("batch")
    me = lax.axis_index("space")
    total = parties * batches
    mine = b * parties + me
    shift = width_y * 4
    tiles = 2 * REACH + 1

    barrier = pltpu.get_barrier_semaphore()

    def greet(k, carry):
        other = lax.rem(mine + k, total)
        pl.semaphore_signal(
            barrier, inc=1, device_id=(other // parties, lax.rem(other, parties)), device_id_type=MESH
        )
        return carry

    lax.fori_loop(1, total, greet, 0)

    vbuf[0:steps, :] = tra[...]
    vbuf[steps : steps + 1, :] = t_cell[...].astype(F32)
    owners = t_own[...]
    match = (lax.broadcasted_iota(I32, (parties, rows), 0) == owners).astype(F32)
    before = lax.broadcasted_iota(I32, (rows, rows), 0) < lax.broadcasted_iota(I32, (rows, rows), 1)
    ahead = dot(match.astype(BF16), before.astype(F32).astype(BF16))
    rank = jnp.sum(match * ahead, axis=0, keepdims=True)
    slot = owners * cap + rank.astype(I32)
    slots = parties * cap
    chosen = (lax.broadcasted_iota(I32, (slots, rows), 0) == slot).astype(F32).astype(BF16)
    values = vbuf[...]
    v_high = values.astype(BF16).astype(F32)
    pieces = jnp.concatenate([v_high, values - v_high], axis=0).astype(BF16)
    sorted_two = dot_lanes(pieces, chosen)
    ordered = sorted_two[:8] + sorted_two[8:]
    group = 128 // cap
    spot = lax.rem(me, group)
    lanes = lax.broadcasted_iota(I32, (8, 128), 1)
    keep = (lanes // cap) == spot
    for dest in range(parties):
        four = ordered[:, (dest // group) * 128 : (dest // group) * 128 + 128]
        turned = pltpu.roll(four, lax.rem(spot - dest % group + group, group) * cap, 1)
        sbuf[dest] = jnp.where(keep, turned, 0.0)
    rbuf[me] = sbuf[me]

    pl.semaphore_wait(barrier, total - 1)

    def route(k):
        dest = lax.rem(me + k, parties)
        return pltpu.make_async_remote_copy(
            src_ref=sbuf.at[dest], dst_ref=rbuf.at[me], send_sem=a2a_s.at[dest],
            recv_sem=a2a_r.at[me], device_id=(b, dest), device_id_type=MESH,
        )

    def arrive(k):
        origin = lax.rem(me + k, parties)
        return pltpu.make_async_remote_copy(
            src_ref=sbuf.at[origin], dst_ref=rbuf.at[origin], send_sem=a2a_s.at[origin],
            recv_sem=a2a_r.at[origin], device_id=(b, origin), device_id_type=MESH,
        )

    def start_route(k, carry):
        route(k).start()
        return carry

    lax.fori_loop(1, parties, start_route, 0)

    def cour_copy(n, hop, receiving):
        part = block
        lo = 0
        if abs(hop) == REACH:
            part = block // 2
            lo = block // 2 if hop > 0 else 0
        at = REACH - hop
        return pltpu.make_async_remote_copy(
            src_ref=cour.at[pl.ds(lo, part)], dst_ref=cext.at[pl.ds(at * block + lo, part)],
            send_sem=c_s.at[n], recv_sem=c_r.at[at],
            device_id=(b, me - hop if receiving else me + hop), device_id_type=MESH,
        )

    def relay_copy(n, hop, receiving):
        at = REACH - hop
        return pltpu.make_async_remote_copy(
            src_ref=relay.at[REACH], dst_ref=relay.at[at], send_sem=l_s.at[n],
            recv_sem=l_r.at[at], device_id=(b, me - hop if receiving else me + hop),
            device_id_type=MESH,
        )

    def inside(place):
        return (place >= 0) & (place < parties)

    for n, hop in enumerate(HOPS):
        @pl.when(inside(me + hop))
        def _():
            cour_copy(n, hop, False).start()

        at = REACH - hop

        @pl.when(jnp.logical_not(inside(me - hop)))
        def _():
            cext[pl.ds(at * block, block), :] = jnp.zeros((block, width_z), F32)
            relay[at] = jnp.zeros(relay.shape[1:], F32)

    cext[pl.ds(REACH * block, block), :] = cour[...]

    i = lax.broadcasted_iota(I32, (block, 2 * block), 0)
    j = lax.broadcasted_iota(I32, (block, 2 * block), 1)
    xi, yi = i // width_y, lax.rem(i, width_y)
    xj, yj = j // width_y - 4, lax.rem(j, width_y)
    along_x = jnp.where(yi == yj, taps_at(jnp.abs(xi - xj), 3.0 * center_tap), 0.0)
    along_y = jnp.where(xi == xj, taps_at(jnp.abs(yi - yj), 0.0), 0.0)
    taps_xy[0], taps_xy[1] = halves_of(along_x + along_y)
    zi = lax.broadcasted_iota(I32, (width_z, width_z), 0)
    zj = lax.broadcasted_iota(I32, (width_z, width_z), 1)
    taps_z[0], taps_z[1] = halves_of(taps_at(jnp.abs(zi - zj), 0.0))

    sources = s_own.shape[1]
    source_row = (s_own[...] - me + REACH) * block + s_cell[...] // width_z
    source_hot = (
        lax.broadcasted_iota(I32, (width_z, sources), 0) == lax.rem(s_cell[...], width_z)
    ).astype(F32).astype(BF16)
    wave = wav[...]
    wave_high = wave.astype(BF16).astype(F32)
    wave_low = wave - wave_high

    def sources_at(t, first, count):
        return placed(
            source_row, wave_high[t : t + 1], wave_low[t : t + 1], source_hot, first, count
        )

    for tile in range(tiles):
        r = pl.ds(tile * block, block)
        start = sources_at(0, tile * block, block)
        ua[r, :] = start
        uh[0, r, :], ul[0, r, :] = halves_of(start)

    def end_arrive(k, carry):
        arrive(k).wait_recv()
        return carry

    lax.fori_loop(1, parties, end_arrive, 0)
    for q in range(slots // 128):
        gathered = rbuf[q * group]
        for s in range(1, group):
            gathered = gathered + rbuf[q * group + s]
        relay[REACH, :, q * 128 : q * 128 + 128] = gathered
    for n, hop in enumerate(HOPS):
        @pl.when(inside(me + hop))
        def _():
            relay_copy(n, hop, False).start()

    last = steps - 1

    def stations(at):
        got = relay[at]
        cell = got[7:8].astype(I32)
        row, column = cell // width_z, lax.rem(cell, width_z)
        hot = (lax.broadcasted_iota(I32, (width_z, slots), 0) == column).astype(F32).astype(BF16)
        high = got.astype(BF16).astype(F32)
        low = got - high
        for t in range(1, steps):
            needed = -(-(t - 1) * 4 // 8)
            if abs(at - REACH) <= needed:
                field_r[t, pl.ds(at * block, block), :] = placed(
                    row, high[t : t + 1], low[t : t + 1], hot, 0, block
                )

    stations(REACH)
    for n, hop in enumerate(HOPS):
        @pl.when(inside(me - hop))
        def _():
            relay_copy(n, hop, True).wait_recv()

        stations(REACH - hop)
    for n, hop in enumerate(HOPS):
        @pl.when(inside(me - hop))
        def _():
            cour_copy(n, hop, True).wait_recv()

    xy_high, xy_low = taps_xy[0], taps_xy[1]
    z_high, z_low = taps_z[0], taps_z[1]

    def laplace(high, low, slot_at, first):
        wide = pl.ds(first - shift, 2 * block)
        own = pl.ds(first, block)
        h, l = high[slot_at, wide, :], low[slot_at, wide, :]
        ho, lo = high[slot_at, own, :], low[slot_at, own, :]
        out = dot(xy_high, h) + dot(xy_low, h) + dot(xy_high, l)
        return out + dot(ho, z_high) + dot(ho, z_low) + dot(lo, z_high)

    for tile in range(2 * tiles - 2):
        r = pl.ds(shift + tile * shift, shift)
        first_b = cext[r, :] * field_r[last, r, :]
        ah[0, r, :], al[0, r, :] = halves_of(first_b)

    fields = (ua, ub)
    adjoints = (aa, ab)
    own = pl.ds(REACH * block, block)
    gradient = None
    for t in range(1, steps):
        now, later = (t - 1) % 2, t % 2
        for tile in range(steps - t):
            first = shift * t + block * tile
            r = pl.ds(first, block)
            change = cext[r, :] * laplace(uh, ul, now, first) + sources_at(t, first, block)
            if first == REACH * block:
                dbuf[t] = change
            elif t % 2 == 1 and abs(first - REACH * block) == shift:
                half = block // 2
                if first < REACH * block:
                    dbuf[t, :half, :] = change[half:]
                else:
                    dbuf[t, half:, :] = change[:half]
            if t < last:
                following = 2.0 * fields[now][r, :] + change
                if t > 1:
                    following = following - fields[later][r, :]
                fields[later][r, :] = following
                uh[later, r, :], ul[later, r, :] = halves_of(following)
        s = last - t
        if s >= 1:
            for tile in range(s):
                first = shift * (steps - s) + block * tile
                r = pl.ds(first, block)
                newer = laplace(ah, al, now, first) + field_r[s, r, :]
                if t == 1:
                    newer = newer + 2.0 * field_r[last, r, :]
                elif t == 2:
                    newer = newer + 2.0 * adjoints[now][r, :] - field_r[last, r, :]
                else:
                    newer = newer + 2.0 * adjoints[now][r, :] - adjoints[later][r, :]
                adjoints[later][r, :] = newer
                if s > 1:
                    ah[later, r, :], al[later, r, :] = halves_of(cext[r, :] * newer)
            field_r[s, own, :] = adjoints[later][own, :]
    for t in range(1, steps):
        term = field_r[t, own, :] * dbuf[t]
        gradient = term if gradient is None else gradient + term

    cells_x = block // width_y
    half_y = width_y // 2
    shaped = gradient.reshape(cells_x, 2, half_y, width_z)
    gbuf[0] = shaped[:, 0]
    gbuf[1] = shaped[:, 1]
    swap = pltpu.make_async_remote_copy(
        src_ref=gbuf.at[1 - b], dst_ref=gin, send_sem=g_s, recv_sem=g_r,
        device_id=(1 - b, me), device_id_type=MESH,
    )
    squares = jnp.sum(gradient * gradient, axis=0, keepdims=True)
    nbuf[mine] = squares[:, :128] + squares[:, 128:]

    def norm_out(k):
        other = lax.rem(mine + k, total)
        return pltpu.make_async_remote_copy(
            src_ref=nbuf.at[mine], dst_ref=nbuf.at[mine], send_sem=n_s.at[other],
            recv_sem=n_r.at[mine], device_id=(other // parties, lax.rem(other, parties)),
            device_id_type=MESH,
        )

    def norm_in(k):
        other = lax.rem(mine + k, total)
        return pltpu.make_async_remote_copy(
            src_ref=nbuf.at[mine], dst_ref=nbuf.at[other], send_sem=n_s.at[other],
            recv_sem=n_r.at[other], device_id=(other // parties, lax.rem(other, parties)),
            device_id_type=MESH,
        )

    def start_norm(k, carry):
        norm_out(k).start()
        return carry

    def end_norm(k, carry):
        norm_in(k).wait_recv()
        return carry

    lax.fori_loop(1, total, start_norm, 0)
    swap.start()

    def end_route(k, carry):
        route(k).wait_send()
        return carry

    lax.fori_loop(1, parties, end_route, 0)
    for n, hop in enumerate(HOPS):
        @pl.when(inside(me + hop))
        def _():
            cour_copy(n, hop, False).wait_send()
            relay_copy(n, hop, False).wait_send()

    lax.fori_loop(1, total, end_norm, 0)
    cells = float(block * width_z * parties)
    mean_first = jnp.sum(jnp.sum(nbuf[0:parties], axis=0), axis=1, keepdims=True) / cells
    mean_second = jnp.sum(jnp.sum(nbuf[parties:total], axis=0), axis=1, keepdims=True) / cells
    scale = 1.0 / jnp.sqrt((mean_first + mean_second) / 2.0 + epsilon)
    agr[...] = jnp.broadcast_to(
        (mean_first + epsilon) / (mean_first + mean_second + 2.0 * epsilon), agr.shape
    )
    swap.wait()
    upd[...] = (gbuf[b] + gin[...]) * scale.reshape(1, 1, 1)

    def end_norm_sent(k, carry):
        norm_out(k).wait_send()
        return carry

    lax.fori_loop(1, total, end_norm_sent, 0)


def body(courant, wavelet, source_owner, source_cell, traces, station_owner, station_cell):
    width_x, width_y, width_z = courant.shape
    rows, steps = traces.shape[1:]
    parties, batches = lax.axis_size("space"), lax.axis_size("batch")
    block = width_x * width_y
    cap = max(2 * rows // parties, 4)
    window = (2 * REACH + 1) * block
    vmem = pl.BlockSpec(memory_space=pltpu.VMEM)
    dma = pltpu.SemaphoreType.DMA
    update, agreement = pl.pallas_call(
        functools.partial(kernel, parties, batches, steps, block, width_y, width_z, cap, rows),
        out_shape=(
            jax.ShapeDtypeStruct((width_x, width_y // 2, width_z), F32),
            jax.ShapeDtypeStruct((1, 128), F32),
        ),
        in_specs=[vmem] * 7,
        out_specs=(vmem, vmem),
        scratch_shapes=[
            pltpu.VMEM((8, rows), F32),
            pltpu.VMEM((parties, 8, 128), F32),
            pltpu.VMEM((parties, 8, 128), F32),
            pltpu.VMEM((2 * REACH + 1, 8, parties * cap), F32),
            pltpu.VMEM((window, width_z), F32),
            pltpu.VMEM((steps, window, width_z), F32),
            pltpu.VMEM((window, width_z), F32),
            pltpu.VMEM((window, width_z), F32),
            pltpu.VMEM((2, window, width_z), BF16),
            pltpu.VMEM((2, window, width_z), BF16),
            pltpu.VMEM((window, width_z), F32),
            pltpu.VMEM((window, width_z), F32),
            pltpu.VMEM((2, window, width_z), BF16),
            pltpu.VMEM((2, window, width_z), BF16),
            pltpu.VMEM((steps, block, width_z), F32),
            pltpu.VMEM((2, block, 2 * block), BF16),
            pltpu.VMEM((2, width_z, width_z), BF16),
            pltpu.VMEM((2, width_x, width_y // 2, width_z), F32),
            pltpu.VMEM((width_x, width_y // 2, width_z), F32),
            pltpu.VMEM((parties * batches, 1, 128), F32),
            dma((parties,)), dma((parties,)),
            dma((6,)), dma((7,)), dma((6,)), dma((7,)),
            dma, dma,
            dma((parties * batches,)), dma((parties * batches,)),
        ],
        compiler_params=pltpu.CompilerParams(
            collective_id=0, has_side_effects=True, vmem_limit_bytes=40 * 1024 * 1024
        ),
    )(
        courant.reshape(block, width_z),
        wavelet[0].T,
        source_owner,
        source_cell,
        traces[0].T,
        station_owner.reshape(1, rows),
        station_cell,
    )
    return update, agreement[0, :1]


def solution(mesh):
    return jax.shard_map(
        body,
        mesh=mesh,
        in_specs=(
            P("space", None, None),
            P("batch", None, None),
            P("batch", None),
            P("batch", None),
            P("batch", "space", None),
            P("batch", "space", None),
            P("batch", "space"),
        ),
        out_specs=(P("space", "batch", None), P()),
        check_vma=False,
    )
```

```python
import functools
import jax
import jax.numpy as jnp
from jax import lax
from jax.experimental import pallas as pl
from jax.experimental.pallas import tpu as pltpu
from jax.sharding import PartitionSpec as P

unit = 5040.0
stencil_taps = (8064.0, -1008.0, 128.0, -9.0)
middle_xy, middle_z = -43008.0, -42.0
epsilon = 1e-06
MESH = pl.DeviceIdType.MESH
F32, BF16, I32 = jnp.float32, jnp.bfloat16, jnp.int32
REACH = 3
HOPS = (-1, 1, -2, 2, -3, 3)


def halves_of(x):
    high = x.astype(BF16)
    return high, (x - high.astype(F32)).astype(BF16)


def dot(a, b):
    return lax.dot_general(a, b, (((1,), (0,)), ((), ())), preferred_element_type=F32)


def dot_lanes(a, b):
    return lax.dot_general(a, b, (((1,), (1,)), ((), ())), preferred_element_type=F32)


def taps_at(distance, middle):
    value = jnp.where(distance == 0, middle, 0.0)
    for k in range(4):
        value = jnp.where(distance == k + 1, stencil_taps[k], value)
    return value


def placed(row_ids, amounts, onehot, first, count):
    rows = lax.broadcasted_iota(I32, (count, row_ids.shape[1]), 0) + first
    here = rows == row_ids
    stacked = [jnp.where(here, part, 0.0).astype(BF16) for pair in amounts for part in pair]
    both = dot_lanes(jnp.concatenate(stacked, axis=0), onehot)
    both = both.reshape(len(amounts), 2, count, both.shape[1])
    return [both[k, 0] + both[k, 1] for k in range(len(amounts))]


def kernel(
    parties, batches, steps, block, width_y, width_z, cap, rows,
    cour_in, wav_in, s_own_in, s_cell_in, tra_in, t_own_in, t_cell_in,
    upd, agr,
    cour, wav, s_own, s_cell, tra, t_own, t_cell, in_s,
    vbuf, sbuf, rbuf, relay, cext, field_r, ua, ub, uh, ul, aa, ab, ah, al, dbuf,
    taps_xy, taps_z, gbuf, gin, nbuf,
    a2a_s, a2a_r, c_s, c_r, l_s, l_r, g_s, g_r, n_s, n_r,
):
    b = lax.axis_index("batch")
    me = lax.axis_index("space")
    total = parties * batches
    mine = b * parties + me
    shift = width_y * 4
    tiles = 2 * REACH + 1

    pairs = (
        (t_own_in, t_own), (t_cell_in, t_cell), (tra_in, tra), (cour_in, cour),
        (wav_in, wav), (s_own_in, s_own), (s_cell_in, s_cell),
    )
    loads = [pltpu.make_async_copy(a, c, in_s.at[k]) for k, (a, c) in enumerate(pairs)]
    for load in loads:
        load.start()

    barrier = pltpu.get_barrier_semaphore()

    def greet(k, carry):
        other = lax.rem(mine + k, total)
        pl.semaphore_signal(
            barrier, inc=1, device_id=(lax.div(other, parties), lax.rem(other, parties)), device_id_type=MESH
        )
        return carry

    lax.fori_loop(1, total, greet, 0)

    for load in loads:
        load.wait()
    for t in range(steps):
        vbuf[t : t + 1, :] = tra[t]
    vbuf[steps : steps + 1, :] = t_cell[...].astype(F32)
    owners = t_own[...]
    match = (lax.broadcasted_iota(I32, (parties, rows), 0) == owners).astype(F32)
    before = lax.broadcasted_iota(I32, (rows, rows), 0) < lax.broadcasted_iota(I32, (rows, rows), 1)
    ahead = dot(match.astype(BF16), before.astype(F32).astype(BF16))
    rank = jnp.sum(match * ahead, axis=0, keepdims=True)
    slot = owners * cap + rank.astype(I32)
    slots = parties * cap
    chosen = (lax.broadcasted_iota(I32, (slots, rows), 0) == slot).astype(F32).astype(BF16)
    values = vbuf[...]
    v_high = values.astype(BF16).astype(F32)
    pieces = jnp.concatenate([v_high, values - v_high], axis=0).astype(BF16)
    sorted_two = dot_lanes(pieces, chosen)
    ordered = sorted_two[:8] + sorted_two[8:]
    group = 128 // cap
    spot = lax.rem(me, group)
    lanes = lax.broadcasted_iota(I32, (8, 128), 1)
    keep = (lanes // cap) == spot
    for dest in range(parties):
        four = ordered[:, (dest // group) * 128 : (dest // group) * 128 + 128]
        turned = pltpu.roll(four, lax.rem(spot - dest % group + group, group) * cap, 1)
        sbuf[dest] = jnp.where(keep, turned, 0.0)
    rbuf[me] = sbuf[me]
    middle = REACH * block
    cext[pl.ds(middle, block), :] = cour[...] * (1.0 / unit)

    pl.semaphore_wait(barrier, total - 1)

    def route(k):
        dest = lax.rem(me + k, parties)
        return pltpu.make_async_remote_copy(
            src_ref=sbuf.at[dest], dst_ref=rbuf.at[me], send_sem=a2a_s.at[dest],
            recv_sem=a2a_r.at[me], device_id=(b, dest), device_id_type=MESH,
        )

    def arrive(k):
        origin = lax.rem(me + k, parties)
        return pltpu.make_async_remote_copy(
            src_ref=sbuf.at[origin], dst_ref=rbuf.at[origin], send_sem=a2a_s.at[origin],
            recv_sem=a2a_r.at[origin], device_id=(b, origin), device_id_type=MESH,
        )

    def start_route(k, carry):
        route(k).start()
        return carry

    lax.fori_loop(1, parties, start_route, 0)

    def cour_copy(n, hop, receiving):
        part = block
        lo = 0
        if abs(hop) == REACH:
            part = block // 2
            lo = block // 2 if hop > 0 else 0
        at = REACH - hop
        return pltpu.make_async_remote_copy(
            src_ref=cext.at[pl.ds(middle + lo, part)], dst_ref=cext.at[pl.ds(at * block + lo, part)],
            send_sem=c_s.at[n], recv_sem=c_r.at[at],
            device_id=(b, me - hop if receiving else me + hop), device_id_type=MESH,
        )

    def relay_copy(n, hop, receiving):
        at = REACH - hop
        return pltpu.make_async_remote_copy(
            src_ref=relay.at[REACH], dst_ref=relay.at[at], send_sem=l_s.at[n],
            recv_sem=l_r.at[at], device_id=(b, me - hop if receiving else me + hop),
            device_id_type=MESH,
        )

    def inside(place):
        return (place >= 0) & (place < parties)

    for n, hop in enumerate(HOPS):
        @pl.when(inside(me + hop))
        def _():
            cour_copy(n, hop, False).start()

        at = REACH - hop

        @pl.when(jnp.logical_not(inside(me - hop)))
        def _():
            cext[pl.ds(at * block, block), :] = jnp.zeros((block, width_z), F32)
            relay[at] = jnp.zeros(relay.shape[1:], F32)

    i = lax.broadcasted_iota(I32, (block, 2 * block), 0)
    j = lax.broadcasted_iota(I32, (block, 2 * block), 1)
    xi, yi = i // width_y, lax.rem(i, width_y)
    xj, yj = j // width_y - 4, lax.rem(j, width_y)
    along_x = jnp.where(yi == yj, taps_at(jnp.abs(xi - xj), middle_xy), 0.0)
    along_y = jnp.where(xi == xj, taps_at(jnp.abs(yi - yj), 0.0), 0.0)
    taps_xy[...] = (along_x + along_y).astype(BF16)
    zi = lax.broadcasted_iota(I32, (width_z, width_z), 0)
    zj = lax.broadcasted_iota(I32, (width_z, width_z), 1)
    taps_z[...] = taps_at(jnp.abs(zi - zj), middle_z).astype(BF16)

    sources = s_own.shape[1]
    source_row = (s_own[...] - me + REACH) * block + s_cell[...] // width_z
    source_hot = (
        lax.broadcasted_iota(I32, (width_z, sources), 0) == lax.rem(s_cell[...], width_z)
    ).astype(F32).astype(BF16)
    def sources_at(t, first, count):
        wave = wav[t]
        wave_high = wave.astype(BF16).astype(F32)
        return placed(
            source_row, [(wave_high, wave - wave_high)], source_hot, first, count
        )[0]

    for tile in range(tiles):
        r = pl.ds(tile * block, block)
        start = sources_at(0, tile * block, block)
        ua[r, :] = start
        uh[0, r, :], ul[0, r, :] = halves_of(start)

    def end_arrive(k, carry):
        arrive(k).wait_recv()
        return carry

    lax.fori_loop(1, parties, end_arrive, 0)
    for q in range(slots // 128):
        gathered = rbuf[q * group]
        for s in range(1, group):
            gathered = gathered + rbuf[q * group + s]
        relay[REACH, :, q * 128 : q * 128 + 128] = gathered
    for n, hop in enumerate(HOPS):
        @pl.when(inside(me + hop))
        def _():
            relay_copy(n, hop, False).start()

    last = steps - 1

    def stations(at):
        got = relay[at]
        cell = got[7:8].astype(I32)
        row, column = cell // width_z, lax.rem(cell, width_z)
        hot = (lax.broadcasted_iota(I32, (width_z, slots), 0) == column).astype(F32).astype(BF16)
        high = got.astype(BF16).astype(F32)
        low = got - high
        times = [t for t in range(1, steps) if abs(at - REACH) <= -(-(t - 1) * 4 // 8)]
        amounts = [(high[t : t + 1], low[t : t + 1]) for t in times]
        for t, field in zip(times, placed(row, amounts, hot, 0, block)):
            field_r[t, pl.ds(at * block, block), :] = field

    stations(REACH)
    for n, hop in enumerate(HOPS):
        @pl.when(inside(me - hop))
        def _():
            relay_copy(n, hop, True).wait_recv()

        stations(REACH - hop)

    def wait_cour(distance):
        for n, hop in enumerate(HOPS):
            if abs(hop) == distance:
                @pl.when(inside(me - hop))
                def _():
                    cour_copy(n, hop, True).wait_recv()

    xy, z = taps_xy[...], taps_z[...]

    def along_z(high, low, slot_at, first, count):
        r = pl.ds(first, count)
        return dot(high[slot_at, r, :], z) + dot(low[slot_at, r, :], z)

    def laplace(high, low, slot_at, first):
        wide = pl.ds(first - shift, 2 * block)
        return dot(xy, high[slot_at, wide, :]) + dot(xy, low[slot_at, wide, :])

    fields = (ua, ub)
    adjoints = (aa, ab)
    own = pl.ds(REACH * block, block)
    gradient = None
    for t in range(1, steps):
        now, later = (t - 1) % 2, t % 2
        start = shift * t
        z_part = along_z(uh, ul, now, start, block * (steps - t))
        order = list(range(steps - t))
        if t == 1:
            order = sorted(order, key=lambda k: abs(2 * k - steps + t + 1))
        for place, tile in enumerate(order):
            if t == 1 and place % 2 == 0:
                wait_cour(place // 2 + 1)
            first = start + block * tile
            r = pl.ds(first, block)
            both = laplace(uh, ul, now, first) + z_part[block * tile : block * tile + block]
            change = cext[r, :] * both + sources_at(t, first, block)
            if first == REACH * block:
                dbuf[t] = change
            elif t % 2 == 1 and abs(first - REACH * block) == shift:
                half = block // 2
                if first < REACH * block:
                    dbuf[t, :half, :] = change[half:]
                else:
                    dbuf[t, half:, :] = change[:half]
            if t < last:
                following = 2.0 * fields[now][r, :] + change
                if t > 1:
                    following = following - fields[later][r, :]
                fields[later][r, :] = following
                uh[later, r, :], ul[later, r, :] = halves_of(following)
        if t == 1:
            for tile in range(2 * tiles - 2):
                r = pl.ds(shift + tile * shift, shift)
                first_b = cext[r, :] * field_r[last, r, :]
                ah[0, r, :], al[0, r, :] = halves_of(first_b)
        s = last - t
        if s >= 1:
            start = shift * (steps - s)
            z_part = along_z(ah, al, now, start, block * s)
            for tile in range(s):
                first = start + block * tile
                r = pl.ds(first, block)
                newer = laplace(ah, al, now, first) + z_part[block * tile : block * tile + block]
                newer = newer + field_r[s, r, :]
                if t == 1:
                    newer = newer + 2.0 * field_r[last, r, :]
                elif t == 2:
                    newer = newer + 2.0 * adjoints[now][r, :] - field_r[last, r, :]
                else:
                    newer = newer + 2.0 * adjoints[now][r, :] - adjoints[later][r, :]
                adjoints[later][r, :] = newer
                if s > 1:
                    ah[later, r, :], al[later, r, :] = halves_of(cext[r, :] * newer)
            field_r[s, own, :] = adjoints[later][own, :]
    for t in range(1, steps):
        term = field_r[t, own, :] * dbuf[t]
        gradient = term if gradient is None else gradient + term

    cells_x = block // width_y
    half_y = width_y // 2
    shaped = gradient.reshape(cells_x, 2, half_y, width_z)
    gbuf[0] = shaped[:, 0]
    gbuf[1] = shaped[:, 1]
    swap = pltpu.make_async_remote_copy(
        src_ref=gbuf.at[1 - b], dst_ref=gin, send_sem=g_s, recv_sem=g_r,
        device_id=(1 - b, me), device_id_type=MESH,
    )
    squares = jnp.sum(gradient * gradient, axis=0, keepdims=True)
    nbuf[mine] = squares[:, :128] + squares[:, 128:]

    def norm_out(k):
        other = lax.rem(mine + k, total)
        return pltpu.make_async_remote_copy(
            src_ref=nbuf.at[mine], dst_ref=nbuf.at[mine], send_sem=n_s.at[other],
            recv_sem=n_r.at[mine], device_id=(lax.div(other, parties), lax.rem(other, parties)),
            device_id_type=MESH,
        )

    def norm_in(k):
        other = lax.rem(mine + k, total)
        return pltpu.make_async_remote_copy(
            src_ref=nbuf.at[mine], dst_ref=nbuf.at[other], send_sem=n_s.at[other],
            recv_sem=n_r.at[other], device_id=(lax.div(other, parties), lax.rem(other, parties)),
            device_id_type=MESH,
        )

    def start_norm(k, carry):
        norm_out(k).start()
        return carry

    def end_norm(k, carry):
        norm_in(k).wait_recv()
        return carry

    lax.fori_loop(1, total, start_norm, 0)
    swap.start()

    def end_route(k, carry):
        route(k).wait_send()
        return carry

    lax.fori_loop(1, parties, end_route, 0)
    for n, hop in enumerate(HOPS):
        @pl.when(inside(me + hop))
        def _():
            cour_copy(n, hop, False).wait_send()
            relay_copy(n, hop, False).wait_send()

    lax.fori_loop(1, total, end_norm, 0)
    cells = float(block * width_z * parties)
    mean_first = jnp.sum(jnp.sum(nbuf[0:parties], axis=0), axis=1, keepdims=True) / cells
    mean_second = jnp.sum(jnp.sum(nbuf[parties:total], axis=0), axis=1, keepdims=True) / cells
    scale = 1.0 / jnp.sqrt((mean_first + mean_second) / 2.0 + epsilon)
    agr[...] = jnp.broadcast_to(
        (mean_first + epsilon) / (mean_first + mean_second + 2.0 * epsilon), agr.shape
    )
    swap.wait()
    upd[...] = (gbuf[b] + gin[...]) * scale.reshape(1, 1, 1)

    def end_norm_sent(k, carry):
        norm_out(k).wait_send()
        return carry

    lax.fori_loop(1, total, end_norm_sent, 0)


def body(courant, wavelet, source_owner, source_cell, traces, station_owner, station_cell):
    width_x, width_y, width_z = courant.shape
    rows, steps = traces.shape[1:]
    parties, batches = lax.axis_size("space"), lax.axis_size("batch")
    block = width_x * width_y
    cap = max(2 * rows // parties, 4)
    window = (2 * REACH + 1) * block
    sources = source_cell.shape[1]
    vmem = pl.BlockSpec(memory_space=pltpu.VMEM)
    hbm = pl.BlockSpec(memory_space=pltpu.HBM)
    dma = pltpu.SemaphoreType.DMA
    update, agreement = pl.pallas_call(
        functools.partial(kernel, parties, batches, steps, block, width_y, width_z, cap, rows),
        out_shape=(
            jax.ShapeDtypeStruct((width_x, width_y // 2, width_z), F32),
            jax.ShapeDtypeStruct((1, 128), F32),
        ),
        in_specs=[hbm] * 7,
        out_specs=(vmem, vmem),
        scratch_shapes=[
            pltpu.VMEM((block, width_z), F32),
            pltpu.VMEM((steps, 1, sources), F32),
            pltpu.VMEM((1, sources), I32),
            pltpu.VMEM((1, sources), I32),
            pltpu.VMEM((steps, 1, rows), F32),
            pltpu.VMEM((1, rows), I32),
            pltpu.VMEM((1, rows), I32),
            dma((7,)),
            pltpu.VMEM((8, rows), F32),
            pltpu.VMEM((parties, 8, 128), F32),
            pltpu.VMEM((parties, 8, 128), F32),
            pltpu.VMEM((2 * REACH + 1, 8, parties * cap), F32),
            pltpu.VMEM((window, width_z), F32),
            pltpu.VMEM((steps, window, width_z), F32),
            pltpu.VMEM((window, width_z), F32),
            pltpu.VMEM((window, width_z), F32),
            pltpu.VMEM((2, window, width_z), BF16),
            pltpu.VMEM((2, window, width_z), BF16),
            pltpu.VMEM((window, width_z), F32),
            pltpu.VMEM((window, width_z), F32),
            pltpu.VMEM((2, window, width_z), BF16),
            pltpu.VMEM((2, window, width_z), BF16),
            pltpu.VMEM((steps, block, width_z), F32),
            pltpu.VMEM((block, 2 * block), BF16),
            pltpu.VMEM((width_z, width_z), BF16),
            pltpu.VMEM((2, width_x, width_y // 2, width_z), F32),
            pltpu.VMEM((width_x, width_y // 2, width_z), F32),
            pltpu.VMEM((parties * batches, 1, 128), F32),
            dma((parties,)), dma((parties,)),
            dma((6,)), dma((7,)), dma((6,)), dma((7,)),
            dma, dma,
            dma((parties * batches,)), dma((parties * batches,)),
        ],
        compiler_params=pltpu.CompilerParams(
            collective_id=0, has_side_effects=True, vmem_limit_bytes=64 * 1024 * 1024
        ),
    )(
        courant.reshape(block, width_z),
        wavelet.transpose(2, 0, 1),
        source_owner,
        source_cell,
        traces.transpose(2, 0, 1),
        station_owner.reshape(1, rows),
        station_cell,
    )
    return update, agreement[0, :1]


def solution(mesh):
    return jax.shard_map(
        body,
        mesh=mesh,
        in_specs=(
            P("space", None, None),
            P("batch", None, None),
            P("batch", None),
            P("batch", None),
            P("batch", "space", None),
            P("batch", "space", None),
            P("batch", "space"),
        ),
        out_specs=(P("space", "batch", None), P()),
        check_vma=False,
    )
```

```python
import functools
import jax
import jax.numpy as jnp
from jax import lax
from jax.experimental import pallas as pl
from jax.experimental.pallas import tpu as pltpu
from jax.sharding import PartitionSpec as P

unit = 5040.0
stencil_taps = (8064.0, -1008.0, 128.0, -9.0)
middle_xy, middle_z = -43008.0, -42.0
epsilon = 1e-06
MESH = pl.DeviceIdType.MESH
F32, BF16, I32 = jnp.float32, jnp.bfloat16, jnp.int32
REACH = 3
HOPS = (-1, 1, -2, 2, -3, 3)


def halves_of(x):
    high = x.astype(BF16)
    return high, (x - high.astype(F32)).astype(BF16)


def dot(a, b):
    return lax.dot_general(a, b, (((1,), (0,)), ((), ())), preferred_element_type=F32)


def dot_lanes(a, b):
    return lax.dot_general(a, b, (((1,), (1,)), ((), ())), preferred_element_type=F32)


def taps_at(distance, middle):
    value = jnp.where(distance == 0, middle, 0.0)
    for k in range(4):
        value = jnp.where(distance == k + 1, stencil_taps[k], value)
    return value


def placed(row_ids, amounts, onehot, first, count):
    rows = lax.broadcasted_iota(I32, (count, row_ids.shape[1]), 0) + first
    here = rows == row_ids
    stacked = [jnp.where(here, part, 0.0).astype(BF16) for pair in amounts for part in pair]
    both = dot_lanes(jnp.concatenate(stacked, axis=0), onehot)
    both = both.reshape(len(amounts), 2, count, both.shape[1])
    return [both[k, 0] + both[k, 1] for k in range(len(amounts))]


def kernel(
    parties, batches, steps, block, width_y, width_z, cap, rows,
    cour_in, wav_in, s_own_in, s_cell_in, tra_in, t_own_in, t_cell_in,
    upd, agr,
    cour, wav, s_own, s_cell, tra, t_own, t_cell, in_s,
    vbuf, sbuf, rbuf, relay, cext, field_r, ua, ub, uh, ul, aa, ab, ah, al, dbuf,
    taps_xy, taps_z, gbuf, gin, nbuf,
    a2a_s, a2a_r, c_s, c_r, l_s, l_r, g_s, g_r, n_s, n_r,
):
    b = lax.axis_index("batch")
    me = lax.axis_index("space")
    total = parties * batches
    mine = b * parties + me
    shift = width_y * 4
    tiles = 2 * REACH + 1

    pairs = (
        (t_own_in, t_own), (t_cell_in, t_cell), (tra_in, tra), (cour_in, cour),
        (wav_in, wav), (s_own_in, s_own), (s_cell_in, s_cell),
    )
    loads = [pltpu.make_async_copy(a, c, in_s.at[k]) for k, (a, c) in enumerate(pairs)]
    for load in loads:
        load.start()

    barrier = pltpu.get_barrier_semaphore()

    def greet(k, carry):
        other = lax.rem(mine + k, total)
        pl.semaphore_signal(
            barrier, inc=1, device_id=(lax.div(other, parties), lax.rem(other, parties)), device_id_type=MESH
        )
        return carry

    lax.fori_loop(1, total, greet, 0)

    for load in loads:
        load.wait()
    for t in range(steps):
        vbuf[t : t + 1, :] = tra[t]
    vbuf[steps : steps + 1, :] = t_cell[...].astype(F32)
    owners = t_own[...]
    match = (lax.broadcasted_iota(I32, (parties, rows), 0) == owners).astype(F32)
    before = lax.broadcasted_iota(I32, (rows, rows), 0) < lax.broadcasted_iota(I32, (rows, rows), 1)
    ahead = dot(match.astype(BF16), before.astype(F32).astype(BF16))
    rank = jnp.sum(match * ahead, axis=0, keepdims=True)
    slot = owners * cap + rank.astype(I32)
    slots = parties * cap
    chosen = (lax.broadcasted_iota(I32, (slots, rows), 0) == slot).astype(F32).astype(BF16)
    values = vbuf[...]
    v_high = values.astype(BF16).astype(F32)
    pieces = jnp.concatenate([v_high, values - v_high], axis=0).astype(BF16)
    sorted_two = dot_lanes(pieces, chosen)
    ordered = sorted_two[:8] + sorted_two[8:]
    group = 128 // cap
    spot = lax.rem(me, group)
    lanes = lax.broadcasted_iota(I32, (8, 128), 1)
    keep = (lanes // cap) == spot
    for dest in range(parties):
        four = ordered[:, (dest // group) * 128 : (dest // group) * 128 + 128]
        turned = pltpu.roll(four, lax.rem(spot - dest % group + group, group) * cap, 1)
        sbuf[dest] = jnp.where(keep, turned, 0.0)
    rbuf[me] = sbuf[me]
    middle = REACH * block
    cext[pl.ds(middle, block), :] = cour[...] * (1.0 / unit)

    pl.semaphore_wait(barrier, total - 1)

    def route(k):
        dest = lax.rem(me + k, parties)
        return pltpu.make_async_remote_copy(
            src_ref=sbuf.at[dest], dst_ref=rbuf.at[me], send_sem=a2a_s.at[dest],
            recv_sem=a2a_r.at[me], device_id=(b, dest), device_id_type=MESH,
        )

    def arrive(k):
        origin = lax.rem(me + k, parties)
        return pltpu.make_async_remote_copy(
            src_ref=sbuf.at[origin], dst_ref=rbuf.at[origin], send_sem=a2a_s.at[origin],
            recv_sem=a2a_r.at[origin], device_id=(b, origin), device_id_type=MESH,
        )

    def start_route(k, carry):
        route(k).start()
        return carry

    lax.fori_loop(1, parties, start_route, 0)

    side = 2 * lax.rem(me, 2) - 1
    partner = me - side
    half = block // 2
    upper = half * (1 - lax.rem(me, 2))

    def inside(place):
        return (place >= 0) & (place < parties)

    def block_copy(n, from_offset, to_offset, lo, count, device):
        start_from = pl.multiple_of((REACH + from_offset) * block + lo, half)
        start_to = pl.multiple_of((REACH + to_offset) * block + lo, half)
        return pltpu.make_async_remote_copy(
            src_ref=cext.at[pl.ds(start_from, count)], dst_ref=cext.at[pl.ds(start_to, count)],
            send_sem=c_s.at[n], recv_sem=c_r.at[n], device_id=(b, device), device_id_type=MESH,
        )

    other_upper = half - upper
    near = (
        me + side, block_copy(0, 0, -side, 0, block, me + side),
        me + side, block_copy(0, 0, side, 0, block, me + side),
    )
    second = (
        me - 2 * side, block_copy(1, 0, 2 * side, 0, block, me - 2 * side),
        me + 2 * side, block_copy(1, 0, 2 * side, 0, block, me + 2 * side),
    )
    third = (
        me + 3 * side, block_copy(2, 0, -3 * side, other_upper, half, me + 3 * side),
        me + 3 * side, block_copy(2, 0, 3 * side, upper, half, me + 3 * side),
    )
    twin = (
        partner, block_copy(3, 0, side, 0, block, partner),
        partner, block_copy(3, 0, -side, 0, block, partner),
    )
    onward = (
        me + side, block_copy(4, side, 2 * side, 0, block, partner),
        me - 2 * side, block_copy(4, 0, -2 * side, 0, block, partner),
    )
    onward_half = (
        me + 2 * side, block_copy(5, 2 * side, 3 * side, upper, half, partner),
        me - 3 * side, block_copy(5, 0, -3 * side, other_upper, half, partner),
    )
    all_copies = (near, second, third, twin, onward, onward_half)

    def send(copy):
        @pl.when(inside(copy[0]))
        def _():
            copy[1].start()

    def receive(copy):
        @pl.when(inside(copy[2]))
        def _():
            copy[3].wait_recv()

    def relay_copy(n, hop, receiving):
        at = REACH - hop
        return pltpu.make_async_remote_copy(
            src_ref=relay.at[REACH], dst_ref=relay.at[at], send_sem=l_s.at[n],
            recv_sem=l_r.at[at], device_id=(b, me - hop if receiving else me + hop),
            device_id_type=MESH,
        )

    send(near)
    send(twin)
    for n, hop in enumerate(HOPS):
        at = REACH - hop

        @pl.when(jnp.logical_not(inside(me - hop)))
        def _():
            cext[pl.ds(at * block, block), :] = jnp.zeros((block, width_z), F32)
            relay[at] = jnp.zeros(relay.shape[1:], F32)

    i = lax.broadcasted_iota(I32, (block, 2 * block), 0)
    j = lax.broadcasted_iota(I32, (block, 2 * block), 1)
    xi, yi = i // width_y, lax.rem(i, width_y)
    xj, yj = j // width_y - 4, lax.rem(j, width_y)
    along_x = jnp.where(yi == yj, taps_at(jnp.abs(xi - xj), middle_xy), 0.0)
    along_y = jnp.where(xi == xj, taps_at(jnp.abs(yi - yj), 0.0), 0.0)
    taps_xy[...] = (along_x + along_y).astype(BF16)
    zi = lax.broadcasted_iota(I32, (width_z, width_z), 0)
    zj = lax.broadcasted_iota(I32, (width_z, width_z), 1)
    taps_z[...] = taps_at(jnp.abs(zi - zj), middle_z).astype(BF16)

    sources = s_own.shape[1]
    source_row = (s_own[...] - me + REACH) * block + s_cell[...] // width_z
    source_hot = (
        lax.broadcasted_iota(I32, (width_z, sources), 0) == lax.rem(s_cell[...], width_z)
    ).astype(F32).astype(BF16)
    def sources_at(t, first, count):
        wave = wav[t]
        wave_high = wave.astype(BF16).astype(F32)
        return placed(
            source_row, [(wave_high, wave - wave_high)], source_hot, first, count
        )[0]

    for tile in range(tiles):
        r = pl.ds(tile * block, block)
        start = sources_at(0, tile * block, block)
        ua[r, :] = start
        uh[0, r, :], ul[0, r, :] = halves_of(start)

    def end_arrive(k, carry):
        arrive(k).wait_recv()
        return carry

    lax.fori_loop(1, parties, end_arrive, 0)
    for q in range(slots // 128):
        gathered = rbuf[q * group]
        for s in range(1, group):
            gathered = gathered + rbuf[q * group + s]
        relay[REACH, :, q * 128 : q * 128 + 128] = gathered
    for n, hop in enumerate(HOPS):
        @pl.when(inside(me + hop))
        def _():
            relay_copy(n, hop, False).start()

    send(second)
    send(third)
    receive(near)
    send(onward)

    last = steps - 1

    def stations(at):
        got = relay[at]
        cell = got[7:8].astype(I32)
        row, column = cell // width_z, lax.rem(cell, width_z)
        hot = (lax.broadcasted_iota(I32, (width_z, slots), 0) == column).astype(F32).astype(BF16)
        high = got.astype(BF16).astype(F32)
        low = got - high
        times = [t for t in range(1, steps) if abs(at - REACH) <= -(-(t - 1) * 4 // 8)]
        amounts = [(high[t : t + 1], low[t : t + 1]) for t in times]
        for t, field in zip(times, placed(row, amounts, hot, 0, block)):
            field_r[t, pl.ds(at * block, block), :] = field

    stations(REACH)
    receive(second)
    send(onward_half)
    for n, hop in enumerate(HOPS):
        @pl.when(inside(me - hop))
        def _():
            relay_copy(n, hop, True).wait_recv()

        stations(REACH - hop)

    def wait_cour(distance):
        for copy in ((twin,), (onward,), (third, onward_half))[distance - 1]:
            receive(copy)

    xy, z = taps_xy[...], taps_z[...]

    def along_z(high, low, slot_at, first, count):
        r = pl.ds(first, count)
        return dot(high[slot_at, r, :], z) + dot(low[slot_at, r, :], z)

    def laplace(high, low, slot_at, first):
        wide = pl.ds(first - shift, 2 * block)
        return dot(xy, high[slot_at, wide, :]) + dot(xy, low[slot_at, wide, :])

    fields = (ua, ub)
    adjoints = (aa, ab)
    own = pl.ds(REACH * block, block)
    gradient = None
    for t in range(1, steps):
        now, later = (t - 1) % 2, t % 2
        start = shift * t
        z_part = along_z(uh, ul, now, start, block * (steps - t))
        order = list(range(steps - t))
        if t == 1:
            order = sorted(order, key=lambda k: abs(2 * k - steps + t + 1))
        for place, tile in enumerate(order):
            if t == 1 and place % 2 == 0:
                wait_cour(place // 2 + 1)
            first = start + block * tile
            r = pl.ds(first, block)
            both = laplace(uh, ul, now, first) + z_part[block * tile : block * tile + block]
            change = cext[r, :] * both + sources_at(t, first, block)
            if first == REACH * block:
                dbuf[t] = change
            elif t % 2 == 1 and abs(first - REACH * block) == shift:
                half = block // 2
                if first < REACH * block:
                    dbuf[t, :half, :] = change[half:]
                else:
                    dbuf[t, half:, :] = change[:half]
            if t < last:
                following = 2.0 * fields[now][r, :] + change
                if t > 1:
                    following = following - fields[later][r, :]
                fields[later][r, :] = following
                uh[later, r, :], ul[later, r, :] = halves_of(following)
        if t == 1:
            for tile in range(2 * tiles - 2):
                r = pl.ds(shift + tile * shift, shift)
                first_b = cext[r, :] * field_r[last, r, :]
                ah[0, r, :], al[0, r, :] = halves_of(first_b)
        s = last - t
        if s >= 1:
            start = shift * (steps - s)
            z_part = along_z(ah, al, now, start, block * s)
            for tile in range(s):
                first = start + block * tile
                r = pl.ds(first, block)
                newer = laplace(ah, al, now, first) + z_part[block * tile : block * tile + block]
                newer = newer + field_r[s, r, :]
                if t == 1:
                    newer = newer + 2.0 * field_r[last, r, :]
                elif t == 2:
                    newer = newer + 2.0 * adjoints[now][r, :] - field_r[last, r, :]
                else:
                    newer = newer + 2.0 * adjoints[now][r, :] - adjoints[later][r, :]
                adjoints[later][r, :] = newer
                if s > 1:
                    ah[later, r, :], al[later, r, :] = halves_of(cext[r, :] * newer)
            field_r[s, own, :] = adjoints[later][own, :]
    for t in range(1, steps):
        term = field_r[t, own, :] * dbuf[t]
        gradient = term if gradient is None else gradient + term

    cells_x = block // width_y
    half_y = width_y // 2
    shaped = gradient.reshape(cells_x, 2, half_y, width_z)
    gbuf[0] = shaped[:, 0]
    gbuf[1] = shaped[:, 1]
    swap = pltpu.make_async_remote_copy(
        src_ref=gbuf.at[1 - b], dst_ref=gin, send_sem=g_s, recv_sem=g_r,
        device_id=(1 - b, me), device_id_type=MESH,
    )
    swap.start()
    squares = jnp.sum(gradient * gradient, axis=0, keepdims=True)
    nbuf[mine] = squares[:, :128] + squares[:, 128:]

    def norm_out(k):
        other = lax.rem(mine + k, total)
        return pltpu.make_async_remote_copy(
            src_ref=nbuf.at[mine], dst_ref=nbuf.at[mine], send_sem=n_s.at[other],
            recv_sem=n_r.at[mine], device_id=(lax.div(other, parties), lax.rem(other, parties)),
            device_id_type=MESH,
        )

    def norm_in(k):
        other = lax.rem(mine + k, total)
        return pltpu.make_async_remote_copy(
            src_ref=nbuf.at[mine], dst_ref=nbuf.at[other], send_sem=n_s.at[other],
            recv_sem=n_r.at[other], device_id=(lax.div(other, parties), lax.rem(other, parties)),
            device_id_type=MESH,
        )

    def start_norm(k, carry):
        norm_out(k).start()
        return carry

    def end_norm(k, carry):
        norm_in(k).wait_recv()
        return carry

    lax.fori_loop(1, total, start_norm, 0)

    def end_route(k, carry):
        route(k).wait_send()
        return carry

    lax.fori_loop(1, parties, end_route, 0)
    for n, hop in enumerate(HOPS):
        @pl.when(inside(me + hop))
        def _():
            relay_copy(n, hop, False).wait_send()
    for copy in all_copies:
        @pl.when(inside(copy[0]))
        def _():
            copy[1].wait_send()

    lax.fori_loop(1, total, end_norm, 0)
    cells = float(block * width_z * parties)
    mean_first = jnp.sum(jnp.sum(nbuf[0:parties], axis=0), axis=1, keepdims=True) / cells
    mean_second = jnp.sum(jnp.sum(nbuf[parties:total], axis=0), axis=1, keepdims=True) / cells
    scale = 1.0 / jnp.sqrt((mean_first + mean_second) / 2.0 + epsilon)
    agr[...] = jnp.broadcast_to(
        (mean_first + epsilon) / (mean_first + mean_second + 2.0 * epsilon), agr.shape
    )
    swap.wait()
    upd[...] = (gbuf[b] + gin[...]) * scale.reshape(1, 1, 1)

    def end_norm_sent(k, carry):
        norm_out(k).wait_send()
        return carry

    lax.fori_loop(1, total, end_norm_sent, 0)


def body(courant, wavelet, source_owner, source_cell, traces, station_owner, station_cell):
    width_x, width_y, width_z = courant.shape
    rows, steps = traces.shape[1:]
    parties, batches = lax.axis_size("space"), lax.axis_size("batch")
    block = width_x * width_y
    cap = max(2 * rows // parties, 4)
    window = (2 * REACH + 1) * block
    sources = source_cell.shape[1]
    vmem = pl.BlockSpec(memory_space=pltpu.VMEM)
    hbm = pl.BlockSpec(memory_space=pltpu.HBM)
    dma = pltpu.SemaphoreType.DMA
    update, agreement = pl.pallas_call(
        functools.partial(kernel, parties, batches, steps, block, width_y, width_z, cap, rows),
        out_shape=(
            jax.ShapeDtypeStruct((width_x, width_y // 2, width_z), F32),
            jax.ShapeDtypeStruct((1, 128), F32),
        ),
        in_specs=[hbm] * 7,
        out_specs=(vmem, vmem),
        scratch_shapes=[
            pltpu.VMEM((block, width_z), F32),
            pltpu.VMEM((steps, 1, sources), F32),
            pltpu.VMEM((1, sources), I32),
            pltpu.VMEM((1, sources), I32),
            pltpu.VMEM((steps, 1, rows), F32),
            pltpu.VMEM((1, rows), I32),
            pltpu.VMEM((1, rows), I32),
            dma((7,)),
            pltpu.VMEM((8, rows), F32),
            pltpu.VMEM((parties, 8, 128), F32),
            pltpu.VMEM((parties, 8, 128), F32),
            pltpu.VMEM((2 * REACH + 1, 8, parties * cap), F32),
            pltpu.VMEM((window, width_z), F32),
            pltpu.VMEM((steps, window, width_z), F32),
            pltpu.VMEM((window, width_z), F32),
            pltpu.VMEM((window, width_z), F32),
            pltpu.VMEM((2, window, width_z), BF16),
            pltpu.VMEM((2, window, width_z), BF16),
            pltpu.VMEM((window, width_z), F32),
            pltpu.VMEM((window, width_z), F32),
            pltpu.VMEM((2, window, width_z), BF16),
            pltpu.VMEM((2, window, width_z), BF16),
            pltpu.VMEM((steps, block, width_z), F32),
            pltpu.VMEM((block, 2 * block), BF16),
            pltpu.VMEM((width_z, width_z), BF16),
            pltpu.VMEM((2, width_x, width_y // 2, width_z), F32),
            pltpu.VMEM((width_x, width_y // 2, width_z), F32),
            pltpu.VMEM((parties * batches, 1, 128), F32),
            dma((parties,)), dma((parties,)),
            dma((6,)), dma((6,)), dma((6,)), dma((7,)),
            dma, dma,
            dma((parties * batches,)), dma((parties * batches,)),
        ],
        compiler_params=pltpu.CompilerParams(
            collective_id=0, has_side_effects=True, vmem_limit_bytes=64 * 1024 * 1024
        ),
    )(
        courant.reshape(block, width_z),
        wavelet.transpose(2, 0, 1),
        source_owner,
        source_cell,
        traces.transpose(2, 0, 1),
        station_owner.reshape(1, rows),
        station_cell,
    )
    return update, agreement[0, :1]


def solution(mesh):
    return jax.shard_map(
        body,
        mesh=mesh,
        in_specs=(
            P("space", None, None),
            P("batch", None, None),
            P("batch", None),
            P("batch", None),
            P("batch", "space", None),
            P("batch", "space", None),
            P("batch", "space"),
        ),
        out_specs=(P("space", "batch", None), P()),
        check_vma=False,
    )
```

```python
import functools
import jax
import jax.numpy as jnp
from jax import lax
from jax.experimental import pallas as pl
from jax.experimental.pallas import tpu as pltpu
from jax.sharding import PartitionSpec as P

unit = 5040.0
stencil_taps = (8064.0, -1008.0, 128.0, -9.0)
middle_xy, middle_z = -43008.0, -42.0
epsilon = 1e-06
MESH = pl.DeviceIdType.MESH
F32, BF16, I32 = jnp.float32, jnp.bfloat16, jnp.int32
REACH = 3
HOPS = (-1, 1, -2, 2, -3, 3)


def halves_of(x):
    high = x.astype(BF16)
    return high, (x - high.astype(F32)).astype(BF16)


def dot(a, b):
    return lax.dot_general(a, b, (((1,), (0,)), ((), ())), preferred_element_type=F32)


def dot_lanes(a, b):
    return lax.dot_general(a, b, (((1,), (1,)), ((), ())), preferred_element_type=F32)


def taps_at(distance, middle):
    value = jnp.where(distance == 0, middle, 0.0)
    for k in range(4):
        value = jnp.where(distance == k + 1, stencil_taps[k], value)
    return value


def placed(row_ids, amounts, onehot, first, count):
    rows = lax.broadcasted_iota(I32, (count, row_ids.shape[1]), 0) + first
    here = rows == row_ids
    stacked = [jnp.where(here, part, 0.0).astype(BF16) for pair in amounts for part in pair]
    both = dot_lanes(jnp.concatenate(stacked, axis=0), onehot)
    both = both.reshape(len(amounts), 2, count, both.shape[1])
    return [both[k, 0] + both[k, 1] for k in range(len(amounts))]


def kernel(
    parties, batches, steps, block, width_y, width_z, cap, rows,
    cour_in, wav_in, s_own_in, s_cell_in, tra_in, t_own_in, t_cell_in,
    upd, agr,
    cour, wav, s_own, s_cell, tra, t_own, t_cell, in_s,
    vbuf, sbuf, rbuf, relay, cext, field_r, ua, ub, uh, ul, aa, ab, ah, al, dbuf,
    taps_xy, taps_z, gbuf, gin, nbuf,
    a2a_s, a2a_r, c_s, c_r, l_s, l_r, g_s, g_r, n_s, n_r,
):
    b = lax.axis_index("batch")
    me = lax.axis_index("space")
    total = parties * batches
    mine = b * parties + me
    shift = width_y * 4
    tiles = 2 * REACH + 1

    pairs = (
        (t_own_in, t_own), (t_cell_in, t_cell), (tra_in, tra), (cour_in, cour),
        (wav_in, wav), (s_own_in, s_own), (s_cell_in, s_cell),
    )
    loads = [pltpu.make_async_copy(a, c, in_s.at[k]) for k, (a, c) in enumerate(pairs)]
    for load in loads:
        load.start()

    barrier = pltpu.get_barrier_semaphore()

    def greet(k, carry):
        other = lax.rem(mine + k, total)
        pl.semaphore_signal(
            barrier, inc=1, device_id=(lax.div(other, parties), lax.rem(other, parties)), device_id_type=MESH
        )
        return carry

    lax.fori_loop(1, total, greet, 0)

    for load in loads:
        load.wait()
    for t in range(steps):
        vbuf[t : t + 1, :] = tra[t]
    vbuf[steps : steps + 1, :] = t_cell[...].astype(F32)
    owners = t_own[...]
    match = (lax.broadcasted_iota(I32, (parties, rows), 0) == owners).astype(F32)
    before = lax.broadcasted_iota(I32, (rows, rows), 0) < lax.broadcasted_iota(I32, (rows, rows), 1)
    ahead = dot(match.astype(BF16), before.astype(F32).astype(BF16))
    rank = jnp.sum(match * ahead, axis=0, keepdims=True)
    slot = owners * cap + rank.astype(I32)
    slots = parties * cap
    chosen = (lax.broadcasted_iota(I32, (slots, rows), 0) == slot).astype(F32).astype(BF16)
    values = vbuf[...]
    v_high = values.astype(BF16).astype(F32)
    pieces = jnp.concatenate([v_high, values - v_high], axis=0).astype(BF16)
    sorted_two = dot_lanes(pieces, chosen)
    ordered = sorted_two[:8] + sorted_two[8:]
    group = 128 // cap
    spot = lax.rem(me, group)
    lanes = lax.broadcasted_iota(I32, (8, 128), 1)
    keep = (lanes // cap) == spot
    for dest in range(parties):
        four = ordered[:, (dest // group) * 128 : (dest // group) * 128 + 128]
        turned = pltpu.roll(four, lax.rem(spot - dest % group + group, group) * cap, 1)
        sbuf[dest] = jnp.where(keep, turned, 0.0)
    rbuf[me] = sbuf[me]
    middle = REACH * block
    cext[pl.ds(middle, block), :] = cour[...] * (1.0 / unit)

    pl.semaphore_wait(barrier, total - 1)

    def route(k):
        dest = lax.rem(me + k, parties)
        return pltpu.make_async_remote_copy(
            src_ref=sbuf.at[dest], dst_ref=rbuf.at[me], send_sem=a2a_s.at[dest],
            recv_sem=a2a_r.at[me], device_id=(b, dest), device_id_type=MESH,
        )

    def arrive(k):
        origin = lax.rem(me + k, parties)
        return pltpu.make_async_remote_copy(
            src_ref=sbuf.at[origin], dst_ref=rbuf.at[origin], send_sem=a2a_s.at[origin],
            recv_sem=a2a_r.at[origin], device_id=(b, origin), device_id_type=MESH,
        )

    def start_route(k, carry):
        route(k).start()
        return carry

    lax.fori_loop(1, parties, start_route, 0)

    side = 2 * lax.rem(me, 2) - 1
    partner = me - side
    half = block // 2
    upper = half * (1 - lax.rem(me, 2))

    def inside(place):
        return (place >= 0) & (place < parties)

    def block_copy(n, from_offset, to_offset, lo, count, device):
        start_from = pl.multiple_of((REACH + from_offset) * block + lo, half)
        start_to = pl.multiple_of((REACH + to_offset) * block + lo, half)
        return pltpu.make_async_remote_copy(
            src_ref=cext.at[pl.ds(start_from, count)], dst_ref=cext.at[pl.ds(start_to, count)],
            send_sem=c_s.at[n], recv_sem=c_r.at[n], device_id=(b, device), device_id_type=MESH,
        )

    other_upper = half - upper
    near = (
        me + side, block_copy(0, 0, -side, 0, block, me + side),
        me + side, block_copy(0, 0, side, 0, block, me + side),
    )
    second = (
        me - 2 * side, block_copy(1, 0, 2 * side, 0, block, me - 2 * side),
        me + 2 * side, block_copy(1, 0, 2 * side, 0, block, me + 2 * side),
    )
    third = (
        me + 3 * side, block_copy(2, 0, -3 * side, other_upper, half, me + 3 * side),
        me + 3 * side, block_copy(2, 0, 3 * side, upper, half, me + 3 * side),
    )
    twin = (
        partner, block_copy(3, 0, side, 0, block, partner),
        partner, block_copy(3, 0, -side, 0, block, partner),
    )
    onward = (
        me + side, block_copy(4, side, 2 * side, 0, block, partner),
        me - 2 * side, block_copy(4, 0, -2 * side, 0, block, partner),
    )
    onward_half = (
        me + 2 * side, block_copy(5, 2 * side, 3 * side, upper, half, partner),
        me - 3 * side, block_copy(5, 0, -3 * side, other_upper, half, partner),
    )
    all_copies = (near, second, third, twin, onward, onward_half)

    def send(copy):
        @pl.when(inside(copy[0]))
        def _():
            copy[1].start()

    def receive(copy):
        @pl.when(inside(copy[2]))
        def _():
            copy[3].wait_recv()

    def relay_copy(n, hop, receiving):
        at = REACH - hop
        return pltpu.make_async_remote_copy(
            src_ref=relay.at[REACH], dst_ref=relay.at[at], send_sem=l_s.at[n],
            recv_sem=l_r.at[at], device_id=(b, me - hop if receiving else me + hop),
            device_id_type=MESH,
        )

    send(near)
    send(twin)
    for n, hop in enumerate(HOPS):
        at = REACH - hop

        @pl.when(jnp.logical_not(inside(me - hop)))
        def _():
            cext[pl.ds(at * block, block), :] = jnp.zeros((block, width_z), F32)
            relay[at] = jnp.zeros(relay.shape[1:], F32)

    i = lax.broadcasted_iota(I32, (block, 2 * block), 0)
    j = lax.broadcasted_iota(I32, (block, 2 * block), 1)
    xi, yi = i // width_y, lax.rem(i, width_y)
    xj, yj = j // width_y - 4, lax.rem(j, width_y)
    along_x = jnp.where(yi == yj, taps_at(jnp.abs(xi - xj), middle_xy), 0.0)
    along_y = jnp.where(xi == xj, taps_at(jnp.abs(yi - yj), 0.0), 0.0)
    taps_xy[...] = (along_x + along_y).astype(BF16)
    zi = lax.broadcasted_iota(I32, (width_z, width_z), 0)
    zj = lax.broadcasted_iota(I32, (width_z, width_z), 1)
    taps_z[...] = taps_at(jnp.abs(zi - zj), middle_z).astype(BF16)

    sources = s_own.shape[1]
    source_row = (s_own[...] - me + REACH) * block + s_cell[...] // width_z
    source_hot = (
        lax.broadcasted_iota(I32, (width_z, sources), 0) == lax.rem(s_cell[...], width_z)
    ).astype(F32).astype(BF16)
    def sources_at(t, first, count):
        wave = wav[t]
        wave_high = wave.astype(BF16).astype(F32)
        return placed(
            source_row, [(wave_high, wave - wave_high)], source_hot, first, count
        )[0]

    for tile in range(tiles):
        r = pl.ds(tile * block, block)
        start = sources_at(0, tile * block, block)
        ua[r, :] = start
        uh[0, r, :], ul[0, r, :] = halves_of(start)

    def end_arrive(k, carry):
        arrive(k).wait_recv()
        return carry

    lax.fori_loop(1, parties, end_arrive, 0)
    for q in range(slots // 128):
        gathered = rbuf[q * group]
        for s in range(1, group):
            gathered = gathered + rbuf[q * group + s]
        relay[REACH, :, q * 128 : q * 128 + 128] = gathered
    for n, hop in enumerate(HOPS):
        @pl.when(inside(me + hop))
        def _():
            relay_copy(n, hop, False).start()

    send(second)
    send(third)
    receive(near)
    send(onward)

    last = steps - 1

    def stations(at):
        got = relay[at]
        cell = got[7:8].astype(I32)
        row, column = cell // width_z, lax.rem(cell, width_z)
        hot = (lax.broadcasted_iota(I32, (width_z, slots), 0) == column).astype(F32).astype(BF16)
        high = got.astype(BF16).astype(F32)
        low = got - high
        times = [t for t in range(1, steps) if abs(at - REACH) <= -(-(t - 1) * 4 // 8)]
        amounts = [(high[t : t + 1], low[t : t + 1]) for t in times]
        for t, field in zip(times, placed(row, amounts, hot, 0, block)):
            field_r[t, pl.ds(at * block, block), :] = field

    stations(REACH)
    receive(second)
    send(onward_half)
    for n, hop in enumerate(HOPS):
        @pl.when(inside(me - hop))
        def _():
            relay_copy(n, hop, True).wait_recv()

        stations(REACH - hop)

    def wait_cour(distance):
        for copy in ((twin,), (onward,), (third, onward_half))[distance - 1]:
            receive(copy)

    xy, z = taps_xy[...], taps_z[...]

    def along_z(high, low, slot_at, first, count):
        r = pl.ds(first, count)
        return dot(high[slot_at, r, :], z) + dot(low[slot_at, r, :], z)

    def laplace(high, low, slot_at, first):
        wide = pl.ds(first - shift, 2 * block)
        return dot(xy, high[slot_at, wide, :]) + dot(xy, low[slot_at, wide, :])

    fields = (ua, ub)
    adjoints = (aa, ab)
    own = pl.ds(REACH * block, block)
    gradient = None
    for t in range(1, steps):
        now, later = (t - 1) % 2, t % 2
        start = shift * t
        z_part = along_z(uh, ul, now, start, block * (steps - t))
        order = list(range(steps - t))
        if t == 1:
            order = sorted(order, key=lambda k: abs(2 * k - steps + t + 1))
        for place, tile in enumerate(order):
            if t == 1 and place % 2 == 0:
                wait_cour(place // 2 + 1)
            first = start + block * tile
            r = pl.ds(first, block)
            both = laplace(uh, ul, now, first) + z_part[block * tile : block * tile + block]
            change = cext[r, :] * both + sources_at(t, first, block)
            if first == REACH * block:
                dbuf[t] = change
            elif t % 2 == 1 and abs(first - REACH * block) == shift:
                half = block // 2
                if first < REACH * block:
                    dbuf[t, :half, :] = change[half:]
                else:
                    dbuf[t, half:, :] = change[:half]
            if t < last:
                following = 2.0 * fields[now][r, :] + change
                if t > 1:
                    following = following - fields[later][r, :]
                fields[later][r, :] = following
                uh[later, r, :], ul[later, r, :] = halves_of(following)
        if t == 1:
            for tile in range(2 * tiles - 2):
                r = pl.ds(shift + tile * shift, shift)
                first_b = cext[r, :] * field_r[last, r, :]
                ah[0, r, :], al[0, r, :] = halves_of(first_b)
        s = last - t
        if s >= 1:
            start = shift * (steps - s)
            z_part = along_z(ah, al, now, start, block * s)
            for tile in range(s):
                first = start + block * tile
                r = pl.ds(first, block)
                newer = laplace(ah, al, now, first) + z_part[block * tile : block * tile + block]
                newer = newer + field_r[s, r, :]
                if t == 1:
                    newer = newer + 2.0 * field_r[last, r, :]
                elif t == 2:
                    newer = newer + 2.0 * adjoints[now][r, :] - field_r[last, r, :]
                else:
                    newer = newer + 2.0 * adjoints[now][r, :] - adjoints[later][r, :]
                adjoints[later][r, :] = newer
                if s > 1:
                    ah[later, r, :], al[later, r, :] = halves_of(cext[r, :] * newer)
            field_r[s, own, :] = adjoints[later][own, :]
    for t in range(1, steps):
        term = field_r[t, own, :] * dbuf[t]
        gradient = term if gradient is None else gradient + term

    cells_x = block // width_y
    half_y = width_y // 2
    shaped = gradient.reshape(cells_x, 2, half_y, width_z)
    gbuf[0] = shaped[:, 0]
    gbuf[1] = shaped[:, 1]
    swap = pltpu.make_async_remote_copy(
        src_ref=gbuf.at[1 - b], dst_ref=gin, send_sem=g_s, recv_sem=g_r,
        device_id=(1 - b, me), device_id_type=MESH,
    )
    swap.start()
    squares = jnp.sum(gradient * gradient, axis=0, keepdims=True)
    nbuf[mine] = squares[:, :128] + squares[:, 128:]

    def norm_out(k):
        other = lax.rem(mine + k, total)
        return pltpu.make_async_remote_copy(
            src_ref=nbuf.at[mine], dst_ref=nbuf.at[mine], send_sem=n_s.at[other],
            recv_sem=n_r.at[mine], device_id=(lax.div(other, parties), lax.rem(other, parties)),
            device_id_type=MESH,
        )

    def norm_in(k):
        other = lax.rem(mine + k, total)
        return pltpu.make_async_remote_copy(
            src_ref=nbuf.at[mine], dst_ref=nbuf.at[other], send_sem=n_s.at[other],
            recv_sem=n_r.at[other], device_id=(lax.div(other, parties), lax.rem(other, parties)),
            device_id_type=MESH,
        )

    def start_norm(k, carry):
        norm_out(k).start()
        return carry

    def end_norm(k, carry):
        norm_in(k).wait_recv()
        return carry

    lax.fori_loop(1, total, start_norm, 0)

    def end_route(k, carry):
        route(k).wait_send()
        return carry

    lax.fori_loop(1, parties, end_route, 0)
    for n, hop in enumerate(HOPS):
        @pl.when(inside(me + hop))
        def _():
            relay_copy(n, hop, False).wait_send()
    for copy in all_copies:
        @pl.when(inside(copy[0]))
        def _():
            copy[1].wait_send()

    lax.fori_loop(1, total, end_norm, 0)
    cells = float(block * width_z * parties)
    mean_first = jnp.sum(jnp.sum(nbuf[0:parties], axis=0), axis=1, keepdims=True) / cells
    mean_second = jnp.sum(jnp.sum(nbuf[parties:total], axis=0), axis=1, keepdims=True) / cells
    scale = 1.0 / jnp.sqrt((mean_first + mean_second) / 2.0 + epsilon)
    share = (mean_first + epsilon) / (mean_first + mean_second + 2.0 * epsilon)
    agr[0:1, :] = jnp.broadcast_to(share, (1, 128))
    agr[1:2, :] = jnp.broadcast_to(scale, (1, 128))
    swap.wait()
    upd[...] = gbuf[b] + gin[...]

    def end_norm_sent(k, carry):
        norm_out(k).wait_send()
        return carry

    lax.fori_loop(1, total, end_norm_sent, 0)


def body(courant, wavelet, source_owner, source_cell, traces, station_owner, station_cell):
    width_x, width_y, width_z = courant.shape
    rows, steps = traces.shape[1:]
    parties, batches = lax.axis_size("space"), lax.axis_size("batch")
    block = width_x * width_y
    cap = max(2 * rows // parties, 4)
    window = (2 * REACH + 1) * block
    sources = source_cell.shape[1]
    vmem = pl.BlockSpec(memory_space=pltpu.VMEM)
    hbm = pl.BlockSpec(memory_space=pltpu.HBM)
    dma = pltpu.SemaphoreType.DMA
    update, agreement = pl.pallas_call(
        functools.partial(kernel, parties, batches, steps, block, width_y, width_z, cap, rows),
        out_shape=(
            jax.ShapeDtypeStruct((width_x, width_y // 2, width_z), F32),
            jax.ShapeDtypeStruct((2, 128), F32),
        ),
        in_specs=[hbm] * 7,
        out_specs=(vmem, vmem),
        scratch_shapes=[
            pltpu.VMEM((block, width_z), F32),
            pltpu.VMEM((steps, 1, sources), F32),
            pltpu.VMEM((1, sources), I32),
            pltpu.VMEM((1, sources), I32),
            pltpu.VMEM((steps, 1, rows), F32),
            pltpu.VMEM((1, rows), I32),
            pltpu.VMEM((1, rows), I32),
            dma((7,)),
            pltpu.VMEM((8, rows), F32),
            pltpu.VMEM((parties, 8, 128), F32),
            pltpu.VMEM((parties, 8, 128), F32),
            pltpu.VMEM((2 * REACH + 1, 8, parties * cap), F32),
            pltpu.VMEM((window, width_z), F32),
            pltpu.VMEM((steps, window, width_z), F32),
            pltpu.VMEM((window, width_z), F32),
            pltpu.VMEM((window, width_z), F32),
            pltpu.VMEM((2, window, width_z), BF16),
            pltpu.VMEM((2, window, width_z), BF16),
            pltpu.VMEM((window, width_z), F32),
            pltpu.VMEM((window, width_z), F32),
            pltpu.VMEM((2, window, width_z), BF16),
            pltpu.VMEM((2, window, width_z), BF16),
            pltpu.VMEM((steps, block, width_z), F32),
            pltpu.VMEM((block, 2 * block), BF16),
            pltpu.VMEM((width_z, width_z), BF16),
            pltpu.VMEM((2, width_x, width_y // 2, width_z), F32),
            pltpu.VMEM((width_x, width_y // 2, width_z), F32),
            pltpu.VMEM((parties * batches, 1, 128), F32),
            dma((parties,)), dma((parties,)),
            dma((6,)), dma((6,)), dma((6,)), dma((7,)),
            dma, dma,
            dma((parties * batches,)), dma((parties * batches,)),
        ],
        compiler_params=pltpu.CompilerParams(
            collective_id=0, has_side_effects=True, vmem_limit_bytes=64 * 1024 * 1024
        ),
    )(
        courant.reshape(block, width_z),
        wavelet.transpose(2, 0, 1),
        source_owner,
        source_cell,
        traces.transpose(2, 0, 1),
        station_owner.reshape(1, rows),
        station_cell,
    )
    return update * agreement[1, 0], agreement[0, :1]


def solution(mesh):
    return jax.shard_map(
        body,
        mesh=mesh,
        in_specs=(
            P("space", None, None),
            P("batch", None, None),
            P("batch", None),
            P("batch", None),
            P("batch", "space", None),
            P("batch", "space", None),
            P("batch", "space"),
        ),
        out_specs=(P("space", "batch", None), P()),
        check_vma=False,
    )
```
